128 devices in a mesh: cols: 16 (over x_hi, y, core), rows: 8 (over z, x_lo).
Axes of the slice: x: 4 (x_hi: 2, x_lo: 2; x = x_hi * 2 + x_lo), y: 4, z: 4, core: 2. Of those that a mesh axis runs over, the one named last changes fastest.
Arguments:
- weight: float32 [8192, 28672], P('rows', 'cols'), may hold values from -6 to 6
- scales: float32 [8192], P('rows'), may hold values from 0.2 to 0.5
- panels: float32 [2048, 28672], P('cols', 'rows')
- block_inverse: float32 [2, 128, 128], replicated
- grid_codes: int32 [16], replicated, may hold values from -12 to 12, as said below
- block_starts: int32 [2], replicated, may hold values from 0 to 26880, as said below
Outputs:
- result: float32 [8192, 28672], P('rows', 'cols')
The draws below stay inside these ranges and needn't reach their ends.
Inputs may be any that keep to these rules, and one draw needn't show every extreme that they name: `grid_codes`: strictly increasing. `block_starts`: strictly increasing multiples of 1792; the last block starts at the last device's columns.
All inputs are finite; a program needn't handle non-finite values.
Results may differ from the reference program's by a relative error of at most 0.00012.
Values sent between devices are 32-bit elements; how exact they have to be, the bound alone decides.
No kernel may reach another device: no remote copies, remote signals or barrier semaphores. Data moves between devices by JAX's collectives and lax.ppermute only.
A program may use at most 128 MiB of HBM per device.

```python
import math
import jax
import jax.numpy as jnp
from jax import lax

OUT = 8192
COLS_IN = 28672
BLK = 128
SUB = 32
LEVELS = 16
BLOCKS = 2
COLS_DEV = 1792
PANELS = 2048
N_COLS = 16


def draw_panels(key, part):
    row_ids = jnp.arange(PANELS, dtype=jnp.int32)[:, None]
    column_ids = jnp.arange(COLS_IN, dtype=jnp.int32)[None, :]
    start_col = row_ids // BLK * COLS_DEV
    local_row = row_ids % BLK
    inside = column_ids - start_col
    noise = jax.random.normal(jax.random.fold_in(key, 11), (PANELS, COLS_IN), jnp.float32)
    diag_vals = jnp.exp(jax.random.uniform(jax.random.fold_in(key, 12), (PANELS, COLS_IN), jnp.float32, -0.7, 0.7))
    upper = jnp.where(inside > local_row, noise / BLK ** 0.5, 0.0)
    upper = jnp.where(inside == local_row, diag_vals, upper)
    values = jnp.where(inside >= BLK, 2.0 * noise / BLK ** 0.5, upper)
    values = jnp.where(inside < 0, 0.0, values)
    return values.astype(jnp.float32)


def draw_block_inverse(key, part):
    noise = jax.random.normal(jax.random.fold_in(key, 21), (BLOCKS, BLK, BLK), jnp.float32)
    diag_vals = jax.random.uniform(jax.random.fold_in(key, 22), (BLOCKS, BLK, BLK), jnp.float32, 0.5, 1.5)
    row_ids = jnp.arange(BLK, dtype=jnp.int32)[:, None]
    column_ids = jnp.arange(BLK, dtype=jnp.int32)[None, :]
    values = jnp.where(column_ids > row_ids, 0.6 * noise / BLK ** 0.5, 0.0)
    values = jnp.where(column_ids == row_ids, diag_vals, values)
    return values.astype(jnp.float32)


def draw_grid_codes(key, part):
    picked = jax.random.permutation(jax.random.fold_in(key, 31), 25)[:LEVELS]
    return (jnp.sort(picked) - 12).astype(jnp.int32)


def draw_block_starts(key, part):
    earlier = jnp.sort(jax.random.permutation(jax.random.fold_in(key, 41), N_COLS - 1)[:BLOCKS - 1])
    owners = jnp.concatenate([earlier.astype(jnp.int32), jnp.full((1,), N_COLS - 1, jnp.int32)])
    return (owners * COLS_DEV).astype(jnp.int32)


def block_scale(rng, dims, cuts, low, high):
    gain, own = 1.0, jax.random.fold_in(rng, 6)
    for axis_at, blocks in cuts:
        draws = jnp.exp(jax.random.uniform(jax.random.fold_in(own, axis_at), (blocks,), jnp.float32, low / len(cuts), high / len(cuts)))
        gain = gain * jnp.repeat(draws, dims[axis_at] // blocks).reshape([-1 if axis == axis_at else 1 for axis in range(len(dims))])
    return gain


def normal_values(rng, dims, width, reach, split=(), kind=jnp.bfloat16):
    values = width * jax.random.normal(rng, dims, jnp.float32)
    if split:
        values = values * block_scale(rng, dims, split, -0.22, 0.18)
    return jnp.clip(values, -reach, reach).astype(kind)


def setup_inputs(seed: int = 0) -> dict:
    arg_keys = jax.random.split(jax.random.key(seed), 7)
    return {
        "weight": normal_values(arg_keys[0], (OUT, COLS_IN), 1.0, 6.0, ((0, 8), (1, 16)), jnp.float32),
        "scales": jnp.clip(jnp.exp(math.log(0.5) - 0.9162907 * jax.random.uniform(arg_keys[1], (OUT,), jnp.float32) ** block_scale(arg_keys[1], (OUT,), ((0, 8),), -0.2, 0.2)), 0.2, 0.5),
        "panels": draw_panels(jax.random.fold_in(arg_keys[6], 71), 0),
        "block_inverse": draw_block_inverse(jax.random.fold_in(arg_keys[6], 71), 0),
        "grid_codes": draw_grid_codes(jax.random.fold_in(arg_keys[6], 71), 0),
        "block_starts": draw_block_starts(jax.random.fold_in(arg_keys[6], 71), 0),
    }


softness = 0.2


def quantize(values, scales, grid_codes):
    levels = grid_codes.astype(jnp.float32)
    ratio = values / scales[:, None]
    output = jnp.zeros_like(values) + levels[0]
    for level_id in range(LEVELS - 1):
        level_gap = levels[level_id + 1] - levels[level_id]
        midpoint = 0.5 * (levels[level_id] + levels[level_id + 1])
        output = output + level_gap * jax.nn.sigmoid((ratio - midpoint) / softness)
    return output * scales[:, None]


def inner_block(block_cols, diag_block, inverse, scales, grid_codes):
    local_ids = jnp.arange(BLK, dtype=jnp.int32)
    pieces = []
    for piece_id in range(BLK // SUB):
        low_col = piece_id * SUB
        current = block_cols[:, low_col:low_col + SUB]
        quantized = quantize(current, scales, grid_codes)
        error_part = jnp.dot(current - quantized, inverse[low_col:low_col + SUB, low_col:low_col + SUB], precision=lax.Precision.HIGHEST, preferred_element_type=jnp.float32)
        later_rows = jnp.where(local_ids[None, :] >= low_col + SUB, diag_block[low_col:low_col + SUB, :], 0.0)
        block_cols = block_cols - jnp.dot(error_part, later_rows, precision=lax.Precision.HIGHEST, preferred_element_type=jnp.float32)
        block_cols = block_cols.at[:, low_col:low_col + SUB].set(quantized)
        pieces.append(error_part)
    return block_cols, jnp.concatenate(pieces, axis=1)


def reference(weight, scales, panels, block_inverse, grid_codes, block_starts):
    cols_per = COLS_IN // N_COLS
    column_ids = jnp.arange(COLS_IN, dtype=jnp.int32)
    for block_id in range(BLOCKS):
        start_col = block_starts[block_id].astype(jnp.int32)
        owner_id = (start_col // cols_per).astype(jnp.int32)
        panel_rows = lax.dynamic_slice_in_dim(panels, (owner_id * BLK).astype(jnp.int32), BLK, 0)
        diag_block = lax.dynamic_slice_in_dim(panel_rows, start_col, BLK, 1)
        block_cols = lax.dynamic_slice_in_dim(weight, start_col, BLK, 1)
        block_cols, errors = inner_block(block_cols, diag_block, block_inverse[block_id], scales, grid_codes)
        weight = lax.dynamic_update_slice_in_dim(weight, block_cols, start_col, 1)
        trail_rows = jnp.where(column_ids[None, :] >= start_col + BLK, panel_rows, 0.0)
        weight = weight - jnp.dot(errors, trail_rows, precision=lax.Precision.HIGHEST, preferred_element_type=jnp.float32)
    return weight
```

```python
import jax
import jax.numpy as jnp
from jax import lax
from jax.experimental import pallas as pl
from jax.experimental.pallas import tpu as pltpu
from jax.sharding import Mesh
from jax.sharding import PartitionSpec as P

BLK = 128
SUB = 32
LEVELS = 16
softness = 0.2

SIZES = (2, 4, 2, 4, 2)
AXES = ("xh", "y", "k", "z", "xl")
COLS = ("xh", "y", "k")
ROWS = ("z", "xl")
CHIPS = ("xh", "y")
N_CHIPS = 8
N_ROWS = 8
LANES = 256
VMEM = 48 * 1024 * 1024


def dot(a, b):
    return jnp.dot(a, b, precision=lax.Precision.HIGHEST, preferred_element_type=jnp.float32)


def fast_dot(a, b):
    return jnp.dot(a, b, preferred_element_type=jnp.float32)


def split(value):
    high = value.astype(jnp.bfloat16)
    low = (value - high.astype(jnp.float32)).astype(jnp.bfloat16)
    return high, low


def quantize(values, steps, inverse_steps, codes):
    levels = [codes[i].astype(jnp.float32) for i in range(LEVELS)]
    scaled = values * (inverse_steps * (0.5 / softness))
    output = jnp.full(values.shape, 0.5 * (levels[0] + levels[-1]), jnp.float32)
    for i in range(LEVELS - 1):
        half_gap = 0.5 * (levels[i + 1] - levels[i])
        shift = (levels[i] + levels[i + 1]) * (0.25 / softness)
        output = output + half_gap * jnp.tanh(scaled - shift)
    return output * steps


def inner_block(parts, steps, diag, inverse, codes):
    diag_t, inverse_t = diag.T, inverse.T
    rounded = [[] for _ in parts]
    errors = [[] for _ in parts]
    parts = list(parts)
    recip = [1.0 / s for s in steps]
    for g in range(BLK // SUB):
        low = g * SUB
        inv_g = inverse_t[low : low + SUB, low : low + SUB]
        later = diag_t[low + SUB :, low : low + SUB]
        for i, part in enumerate(parts):
            current = part[:SUB]
            quantized = quantize(current, steps[i], recip[i], codes)
            error = dot(inv_g, current - quantized)
            rounded[i].append(quantized)
            errors[i].append(error)
            if low + SUB < BLK:
                parts[i] = part[SUB:] - dot(later, error)
    return [jnp.concatenate(r, 0) for r in rounded], [jnp.concatenate(e, 0) for e in errors]


def transposed_parts(tiles):
    per = LANES // BLK
    turned = [t.T for t in tiles]
    return [jnp.concatenate(turned[i : i + per], 1) for i in range(0, len(turned), per)]


def first_kernel(flags, codes, halves_ref, scales_ref, inverse_ref, error_ref, rounded_ref):
    own = flags[0]
    tiles = []
    for half in range(2):
        for q in range(4):
            tiles.append(halves_ref[half, :, q * BLK : (q + 1) * BLK])
    diag = halves_ref[own, :, 4 * BLK : 5 * BLK]
    parts = transposed_parts(tiles)
    steps = [scales_ref[:, i * LANES : (i + 1) * LANES] for i in range(len(parts))]
    rounded, errors = inner_block(parts, steps, diag, inverse_ref[...], codes)
    for i in range(len(parts)):
        rows = slice(i * LANES, (i + 1) * LANES)
        rounded_ref[rows, :] = rounded[i].T
        high, low = split(errors[i].T)
        error_ref[rows, :BLK] = high
        error_ref[rows, BLK:] = low


def last_kernel(
    flags, codes, weight_ref, block_ref, rounded_ref, error_ref, panel_ref, panel1_ref, scales_ref, inverse_ref,
    out_ref, m0_ref, m0_low_ref, m1_ref, m1_low_ref, error1_ref, rounded1_ref,
):
    step = pl.program_id(0)
    after, owner, last = flags[1], flags[2], flags[3]
    rows = out_ref.shape[0]

    def stage(source, masked, pair_ref, low_ref):
        value = source[...]
        ids = lax.broadcasted_iota(jnp.int32, value.shape, 1)
        value = jnp.where(jnp.logical_and(masked == 1, ids < BLK), 0.0, value)
        high, low = split(value)
        pair_ref[:BLK, :] = high
        pair_ref[BLK:, :] = high
        low_ref[...] = low

    def product(error, pair, low):
        return fast_dot(error, pair) + fast_dot(error[:, :BLK], low)

    @pl.when(jnp.logical_and(step == 0, after == 1))
    def _():
        stage(panel_ref, owner, m0_ref, m0_low_ref)

    @pl.when(jnp.logical_and(step == 0, last == 1))
    def _():
        block = block_ref[...] - product(error_ref[...], m0_ref[:, :BLK], m0_low_ref[:, :BLK])
        tiles = [block[i * BLK : (i + 1) * BLK] for i in range(block.shape[0] // BLK)]
        parts = transposed_parts(tiles)
        steps = [scales_ref[:, i * LANES : (i + 1) * LANES] for i in range(len(parts))]
        rounded, errors = inner_block(parts, steps, panel1_ref[:, :BLK], inverse_ref[...], codes)
        for i in range(len(parts)):
            span = slice(i * LANES, (i + 1) * LANES)
            rounded1_ref[span, :] = rounded[i].T
            high, low = split(errors[i].T)
            error1_ref[span, :BLK] = high
            error1_ref[span, BLK:] = low
        stage(panel1_ref, last, m1_ref, m1_low_ref)

    here = pl.ds(pl.multiple_of(step * rows, rows), rows)

    @pl.when(after == 0)
    def _():
        out_ref[...] = weight_ref[...]

    @pl.when(jnp.logical_and(after == 1, last == 0))
    def _():
        out_ref[...] = weight_ref[...] - product(error_ref[here, :], m0_ref[...], m0_low_ref[...])

    @pl.when(last == 1)
    def _():
        out_ref[...] = (
            weight_ref[...]
            - product(error_ref[here, :], m0_ref[...], m0_low_ref[...])
            - product(error1_ref[here, :], m1_ref[...], m1_low_ref[...])
        )
        out_ref[:, :BLK] = rounded1_ref[here, :]

    @pl.when(owner == 1)
    def _():
        out_ref[:, :BLK] = rounded_ref[here, :]


def first_call(flags, codes, halves, scales, inverse):
    n = scales.shape[1]
    smem, vmem = pl.BlockSpec(memory_space=pltpu.SMEM), pl.BlockSpec(memory_space=pltpu.VMEM)
    return pl.pallas_call(
        first_kernel,
        out_shape=(jax.ShapeDtypeStruct((n, 2 * BLK), jnp.bfloat16), jax.ShapeDtypeStruct((n, BLK), jnp.float32)),
        in_specs=[smem, smem, vmem, vmem, vmem],
        out_specs=(vmem, vmem),
        compiler_params=pltpu.CompilerParams(vmem_limit_bytes=VMEM),
        cost_estimate=pl.CostEstimate(flops=10**9, bytes_accessed=2 * 10**6, transcendentals=2 * 10**6),
        name="round_first",
    )(flags, codes, halves, scales, inverse)


def last_call(flags, codes, weight, block, rounded, error, panel, panel1, scales, inverse):
    n, width = weight.shape
    rows = 128
    smem, vmem = pl.BlockSpec(memory_space=pltpu.SMEM), pl.BlockSpec(memory_space=pltpu.VMEM)
    tall = pl.BlockSpec((rows, width), lambda i: (i, 0))
    return pl.pallas_call(
        last_kernel,
        grid=(n // rows,),
        out_shape=jax.ShapeDtypeStruct((n, width), jnp.float32),
        in_specs=[smem, smem, tall, vmem, vmem, vmem, vmem, vmem, vmem, vmem],
        out_specs=tall,
        scratch_shapes=[
            pltpu.VMEM((2 * BLK, width), jnp.bfloat16),
            pltpu.VMEM((BLK, width), jnp.bfloat16),
            pltpu.VMEM((2 * BLK, width), jnp.bfloat16),
            pltpu.VMEM((BLK, width), jnp.bfloat16),
            pltpu.VMEM((n, 2 * BLK), jnp.bfloat16),
            pltpu.VMEM((n, BLK), jnp.float32),
        ],
        compiler_params=pltpu.CompilerParams(vmem_limit_bytes=VMEM),
        cost_estimate=pl.CostEstimate(flops=2 * 10**9, bytes_accessed=16 * 10**6, transcendentals=2 * 10**6),
        name="update_all",
    )(flags, codes, weight, block, rounded, error, panel, panel1, scales, inverse)


def device_at(chip, core, row):
    return (chip * 2 + core) * N_ROWS + row


def local(weight, scales, panels, block_inverse, grid_codes, block_starts):
    width = weight.shape[1]
    xh, y, core, z, xl = (lax.axis_index(a) for a in AXES)
    chip = xh * 4 + y
    row = z * 2 + xl
    col = chip * 2 + core
    owner = block_starts[0] // width
    owner_chip, owner_core = owner // 2, owner % 2
    piece = BLK // N_CHIPS
    swap = [(0, 1), (1, 0)]

    last_chip, last_core, last_row = N_CHIPS - 1, 1, N_ROWS - 1
    panel1 = panels[:, width:]
    for bit in (1, 2, 4):
        pairs = []
        for r in range(N_ROWS):
            if (r ^ last_row) & ~(2 * bit - 1) == 0:
                pairs.append((device_at(last_chip, last_core, r), device_at(last_chip, last_core, r ^ bit)))
        got = lax.ppermute(panel1, AXES, pairs)
        panel1 = jnp.where((row & bit) != 0, panel1, got)

    diag = jnp.where(core == 0, panels[:, :BLK], panels[:, width : width + BLK])
    got = lax.ppermute(diag, "xl", swap)
    diag = jnp.where(xl == (chip & 1), diag, got)
    got = lax.ppermute(diag, "z", [(i, i ^ 1) for i in range(4)])
    diag = jnp.where((z & 1) == ((chip >> 1) & 1), diag, got)
    got = lax.ppermute(diag, "z", [(i, i ^ 2) for i in range(4)])
    diag = jnp.where((z >> 1) == (chip >> 2), diag, got)

    block = weight[:, :BLK]
    half = block.shape[0] // 2
    left, right = panels[:, :width], panels[:, width:]
    top, bottom = block[:half], block[half:]
    got_panel = lax.ppermute(jnp.where(core == 0, right, left), "k", swap)
    got_block = lax.ppermute(jnp.where(core == 0, bottom, top), "k", swap)
    mine = core == owner_core
    panel = jnp.where(mine, jnp.where(core == 0, left, right), got_panel)
    rows_b = jnp.where(mine, jnp.where(core == 0, top, bottom), got_block)
    quarters = [rows_b[q * BLK : (q + 1) * BLK] for q in range(4)]

    sent = jnp.concatenate([panel] + quarters + [diag], axis=1)
    came = lax.all_to_all(sent, CHIPS, 0, 0, tiled=True)
    came = lax.dynamic_slice_in_dim(came, owner_chip * piece, piece, 0)

    pairs = [
        (device_at(d, k, r), device_at(r, k, d)) for d in range(N_CHIPS) for k in range(2) for r in range(N_ROWS)
    ]
    turned = lax.ppermute(came[:, :width], AXES, pairs)

    small = jnp.tile(came[:, width:], (N_CHIPS, 1))
    small = lax.all_to_all(small, CHIPS, 0, 0, tiled=True)
    other = lax.ppermute(small, "k", swap)
    halves = jnp.stack([jnp.where(core == 0, small, other), jnp.where(core == 0, other, small)])

    flags = jnp.stack(
        [
            owner_core,
            (col >= owner).astype(jnp.int32),
            (col == owner).astype(jnp.int32),
            (col == 2 * N_CHIPS - 1).astype(jnp.int32),
        ]
    )
    wide_scales = scales[None, :]
    error, rounded = first_call(flags, grid_codes, halves, wide_scales, block_inverse[0])

    panel0 = lax.all_to_all(jnp.tile(turned, (N_ROWS, 1)), ROWS, 0, 0, tiled=True)
    return last_call(
        flags, grid_codes, weight, block, rounded, error, panel0, panel1, wide_scales, block_inverse[1]
    )


def solution(mesh):
    torus = Mesh(mesh.devices.reshape(SIZES), AXES)
    return jax.shard_map(
        local,
        mesh=torus,
        in_specs=(P(ROWS, COLS), P(ROWS), P(COLS, ROWS), P(), P(), P()),
        out_specs=P(ROWS, COLS),
        check_vma=False,
    )
```

```python
import functools

import jax
import jax.numpy as jnp
from jax import lax
from jax.experimental import pallas as pl
from jax.experimental.pallas import tpu as pltpu
from jax.sharding import Mesh
from jax.sharding import PartitionSpec as P

BLK = 128
SUB = 32
LEVELS = 16
softness = 0.2

SIZES = (2, 4, 2, 4, 2)
AXES = ("xh", "y", "k", "z", "xl")
COLS = ("xh", "y", "k")
ROWS = ("z", "xl")
CHIPS = ("xh", "y")
N_CHIPS = 8
N_ROWS = 8
LANES = 256
VMEM = 16 * 1024 * 1024
WIDE_VMEM = 51 * 1024 * 1024
BIG_VMEM = 54 * 1024 * 1024


def dot(a, b):
    return jnp.dot(a, b, precision=lax.Precision.HIGHEST, preferred_element_type=jnp.float32)


def fast_dot(a, b):
    return jnp.dot(a, b, preferred_element_type=jnp.float32)


def split(value):
    high = value.astype(jnp.bfloat16)
    low = (value - high.astype(jnp.float32)).astype(jnp.bfloat16)
    return high, low


def quantize(values, steps, inverse_steps, codes):
    levels = [codes[i].astype(jnp.float32) for i in range(LEVELS)]
    scaled = values * (inverse_steps * (0.5 / softness))
    output = jnp.full(values.shape, 0.5 * (levels[0] + levels[-1]), jnp.float32)
    for i in range(LEVELS - 1):
        half_gap = 0.5 * (levels[i + 1] - levels[i])
        shift = (levels[i] + levels[i + 1]) * (0.25 / softness)
        output = output + half_gap * jnp.tanh(scaled - shift)
    return output * steps


def inner_block(parts, steps, diag, inverse, codes):
    diag_t, inverse_t = diag.T, inverse.T
    rounded = [[] for _ in parts]
    errors = [[] for _ in parts]
    parts = list(parts)
    recip = [1.0 / s for s in steps]
    for g in range(BLK // SUB):
        low = g * SUB
        inv_g = inverse_t[low : low + SUB, low : low + SUB]
        later = diag_t[low + SUB :, low : low + SUB]
        for i, part in enumerate(parts):
            current = part[:SUB]
            quantized = quantize(current, steps[i], recip[i], codes)
            error = dot(inv_g, current - quantized)
            rounded[i].append(quantized)
            errors[i].append(error)
            if low + SUB < BLK:
                parts[i] = part[SUB:] - dot(later, error)
    return [jnp.concatenate(r, 0) for r in rounded], [jnp.concatenate(e, 0) for e in errors]


def transposed_parts(tiles):
    per = LANES // BLK
    turned = [t.T for t in tiles]
    return [jnp.concatenate(turned[i : i + per], 1) for i in range(0, len(turned), per)]


def first_kernel(flags, codes, small_ref, other_ref, scales_ref, inverse_ref, error_ref, rounded_ref):
    core, mine = flags[4], flags[0]
    half = scales_ref.shape[1] // 2
    parts, steps, places = [], [], []
    for ref, side in ((small_ref, core), (other_ref, 1 - core)):
        tiles = [ref[i : i + BLK, :] for i in range(0, half, BLK)]
        for i, part in enumerate(transposed_parts(tiles)):
            place = pl.multiple_of(side * half + i * LANES, LANES)
            parts.append(part)
            places.append(place)
            steps.append(scales_ref[:, pl.ds(place, LANES)])
    diag = jnp.where(mine == 1, small_ref[half:, :], other_ref[half:, :])
    rounded, errors = inner_block(parts, steps, diag, inverse_ref[...], codes)
    for i, place in enumerate(places):
        rows = pl.ds(place, LANES)
        rounded_ref[rows, :] = rounded[i].T
        high, low = split(errors[i].T)
        error_ref[rows, :BLK] = high
        error_ref[rows, BLK:] = low


def prepare_kernel(panel_ref, block_ref, own_ref, other_ref, diag_ref, one_ref, two_ref):
    core = lax.axis_index("k")
    last = (lax.axis_index("xh") * 4 + lax.axis_index("y")) * 2 + core == 2 * N_CHIPS - 1
    width, half = panel_ref.shape[1] // 2, block_ref.shape[0] // 2

    @pl.when(last)
    def _():
        one_ref[...] = panel_ref[:, width : width + width // 2]
        two_ref[...] = panel_ref[:, width + width // 2 :]

    piece = BLK // N_CHIPS
    for side in range(2):

        @pl.when(core == side)
        def _():
            diag_ref[...] = panel_ref[:, side * width : side * width + BLK]
            for ref, take in ((own_ref, side), (other_ref, 1 - side)):
                ref[:, :width] = panel_ref[:, take * width : (take + 1) * width]
                for q in range(half // BLK):
                    row = take * half + q * BLK
                    ref[:, width + q * BLK : width + (q + 1) * BLK] = block_ref[row : row + BLK, :]


def join_kernel(flags, rows_ref, diag_ref, got_ref, small_ref):
    z, chip = flags[5], flags[6]
    near = lax.div(z, 2) == lax.div(chip, 4)
    n = rows_ref.shape[0]
    small_ref[:n, :] = rows_ref[...]
    small_ref[n:, :] = jnp.where(near, diag_ref[...], got_ref[...])


def copies_kernel(flags, piece_ref, spread_ref):
    for e in range(N_ROWS):
        spread_ref[e] = piece_ref[...]


def choose_kernel(flags, own_ref, got_ref, panel_ref, rows_ref):
    mine, width = flags[0], panel_ref.shape[1]
    for value, ref in ((1, own_ref), (0, got_ref)):

        @pl.when(mine == value)
        def _():
            panel_ref[...] = ref[:, :width]
            for q in range(rows_ref.shape[0] // BLK):
                rows_ref[q * BLK : (q + 1) * BLK, :] = ref[:, width + q * BLK : width + (q + 1) * BLK]


def small_call(kernel, name, shapes, flags, *arrays, flops=0):
    smem, vmem = pl.BlockSpec(memory_space=pltpu.SMEM), pl.BlockSpec(memory_space=pltpu.VMEM)
    return pl.pallas_call(
        kernel,
        out_shape=tuple(jax.ShapeDtypeStruct(shape, jnp.float32) for shape in shapes),
        in_specs=[smem] + [vmem] * len(arrays),
        out_specs=(vmem,) * len(shapes),
        compiler_params=pltpu.CompilerParams(vmem_limit_bytes=VMEM),
        cost_estimate=pl.CostEstimate(flops=flops, bytes_accessed=10**5, transcendentals=0),
        name=name,
    )(flags, *arrays)


def prepare_call(panels, weight):
    n, wide = panels.shape
    rows = weight.shape[0]
    tall = wide // 2 + rows // 2
    whole = lambda shape: pl.BlockSpec(shape, lambda i: (0, 0))
    return pl.pallas_call(
        prepare_kernel,
        grid=(1,),
        out_shape=tuple(jax.ShapeDtypeStruct(s, jnp.float32) for s in ((n, tall), (n, tall), (n, BLK), (n, wide // 4), (n, wide // 4))),
        in_specs=[whole((n, wide)), whole((rows, BLK))],
        out_specs=(whole((n, tall)), whole((n, tall)), whole((n, BLK)), whole((n, wide // 4)), whole((n, wide // 4))),
        compiler_params=pltpu.CompilerParams(vmem_limit_bytes=BIG_VMEM),
        name="halves",
    )(panels, weight)


def last_kernel(
    flags, codes, weight_hbm, rounded_ref, error_ref, panel_ref, one_hbm, got_one_hbm, two_hbm, got_two_hbm, scales_ref, inverse_ref,
    out_ref, m0_ref, m0_low_ref, m1_ref, m1_low_ref, error1_ref, rounded1_ref, weight_ref, arrived, panel1_ref, block_ref, down_done,
):
    step = pl.program_id(0)
    after, owner, last = flags[1], flags[2], flags[3]
    rows = out_ref.shape[0]

    def read(i):
        span = pl.ds(pl.multiple_of(i * rows, rows), rows)
        return pltpu.make_async_copy(weight_hbm.at[span, :], weight_ref.at[span, :], arrived.at[i])

    block_read = pltpu.make_async_copy(weight_hbm.at[:, :BLK], block_ref, down_done.at[1])

    @pl.when(jnp.logical_and(step == 0, last == 1))
    def _():
        block_read.start()

    half = out_ref.shape[1] // 2
    left, right = panel1_ref.at[:, :half], panel1_ref.at[:, half:]
    for bit, kept, got, place, at in ((4, one_hbm, got_one_hbm, left, 0), (1, two_hbm, got_two_hbm, right, 2)):
        for held, source in ((True, kept), (False, got)):

            @pl.when(jnp.logical_and(jnp.logical_and(step == 0, last == 1), ((flags[8] & bit) != 0) == held))
            def _():
                pltpu.make_async_copy(source, place, down_done.at[at]).start()

    @pl.when(step == 0)
    def _():
        for i in range(weight_hbm.shape[0] // rows):
            read(i).start()

    def stage(source, masked, pair_ref, low_ref):
        value = source[...]
        ids = lax.broadcasted_iota(jnp.int32, value.shape, 1)
        value = jnp.where(jnp.logical_and(masked == 1, ids < BLK), 0.0, value)
        high, low = split(value)
        pair_ref[:BLK, :] = high
        pair_ref[BLK:, :] = high
        low_ref[...] = low

    def product(error, pair, low):
        return fast_dot(error, pair) + fast_dot(error[:, :BLK], low)

    @pl.when(jnp.logical_and(step == 0, after == 1))
    def _():
        stage(panel_ref, owner, m0_ref, m0_low_ref)

    @pl.when(jnp.logical_and(step == 0, last == 1))
    def _():
        pltpu.make_async_copy(one_hbm, left, down_done.at[0]).wait()
        pltpu.make_async_copy(two_hbm, right, down_done.at[2]).wait()
        block_read.wait()
        block = block_ref[...] - product(error_ref[...], m0_ref[:, :BLK], m0_low_ref[:, :BLK])
        tiles = [block[i * BLK : (i + 1) * BLK] for i in range(block.shape[0] // BLK)]
        parts = transposed_parts(tiles)
        steps = [scales_ref[:, i * LANES : (i + 1) * LANES] for i in range(len(parts))]
        rounded, errors = inner_block(parts, steps, panel1_ref[:, :BLK], inverse_ref[...], codes)
        for i in range(len(parts)):
            span = slice(i * LANES, (i + 1) * LANES)
            rounded1_ref[span, :] = rounded[i].T
            high, low = split(errors[i].T)
            error1_ref[span, :BLK] = high
            error1_ref[span, BLK:] = low
        stage(panel1_ref, last, m1_ref, m1_low_ref)

    here = pl.ds(pl.multiple_of(step * rows, rows), rows)
    read(step).wait()

    @pl.when(after == 0)
    def _():
        out_ref[...] = weight_ref[here, :]

    @pl.when(jnp.logical_and(after == 1, last == 0))
    def _():
        out_ref[...] = weight_ref[here, :] - product(error_ref[here, :], m0_ref[...], m0_low_ref[...])

    @pl.when(last == 1)
    def _():
        out_ref[...] = (
            weight_ref[here, :]
            - product(error_ref[here, :], m0_ref[...], m0_low_ref[...])
            - product(error1_ref[here, :], m1_ref[...], m1_low_ref[...])
        )
        out_ref[:, :BLK] = rounded1_ref[here, :]

    @pl.when(owner == 1)
    def _():
        out_ref[:, :BLK] = rounded_ref[here, :]


def first_call(flags, codes, small, other, scales, inverse):
    n = scales.shape[1]
    smem, vmem = pl.BlockSpec(memory_space=pltpu.SMEM), pl.BlockSpec(memory_space=pltpu.VMEM)
    return pl.pallas_call(
        first_kernel,
        out_shape=(jax.ShapeDtypeStruct((n, 2 * BLK), jnp.bfloat16), jax.ShapeDtypeStruct((n, BLK), jnp.float32)),
        in_specs=[smem, smem, vmem, vmem, vmem, vmem],
        out_specs=(vmem, vmem),
        compiler_params=pltpu.CompilerParams(vmem_limit_bytes=VMEM),
        cost_estimate=pl.CostEstimate(flops=0, bytes_accessed=10**5, transcendentals=0),
        name="round_first",
    )(flags, codes, small, other, scales, inverse)


def last_call(flags, codes, weight, rounded, error, panel, panel1, scales, inverse):
    n, width = weight.shape
    rows = 256
    smem, vmem = pl.BlockSpec(memory_space=pltpu.SMEM), pl.BlockSpec(memory_space=pltpu.VMEM)
    tall, hbm = pl.BlockSpec((rows, width), lambda i: (i, 0)), pl.BlockSpec(memory_space=pltpu.HBM)
    return pl.pallas_call(
        last_kernel,
        grid=(n // rows,),
        out_shape=jax.ShapeDtypeStruct((n, width), jnp.float32),
        in_specs=[smem, smem, hbm] + [vmem] * 3 + [hbm] * 4 + [vmem] * 2,
        out_specs=tall,
        scratch_shapes=[
            pltpu.VMEM((2 * BLK, width), jnp.bfloat16),
            pltpu.VMEM((BLK, width), jnp.bfloat16),
            pltpu.VMEM((2 * BLK, width), jnp.bfloat16),
            pltpu.VMEM((BLK, width), jnp.bfloat16),
            pltpu.VMEM((n, 2 * BLK), jnp.bfloat16),
            pltpu.VMEM((n, BLK), jnp.float32),
            pltpu.VMEM((n, width), jnp.float32),
            pltpu.SemaphoreType.DMA((n // rows,)),
            pltpu.VMEM((BLK, width), jnp.float32),
            pltpu.VMEM((n, BLK), jnp.float32),
            pltpu.SemaphoreType.DMA((3,)),
        ],
        compiler_params=pltpu.CompilerParams(vmem_limit_bytes=WIDE_VMEM),
        cost_estimate=pl.CostEstimate(flops=2 * 10**9, bytes_accessed=16 * 10**6, transcendentals=2 * 10**6),
        name="update_all",
    )(flags, codes, weight, rounded, error, panel, *panel1, scales, inverse)


def device_at(chip, core, row):
    return (chip * 2 + core) * N_ROWS + row


def local(weight, scales, panels, block_inverse, grid_codes, block_starts):
    width = weight.shape[1]
    xh, y, core, z, xl = (lax.axis_index(a) for a in AXES)
    chip = xh * 4 + y
    row = z * 2 + xl
    col = chip * 2 + core
    owner = block_starts[0] // width
    owner_chip, owner_core = owner // 2, owner % 2
    mine = core == owner_core
    piece = BLK // N_CHIPS
    swap = [(0, 1), (1, 0)]
    flags = jnp.stack(
        [
            mine.astype(jnp.int32),
            (col >= owner).astype(jnp.int32),
            (col == owner).astype(jnp.int32),
            (col == 2 * N_CHIPS - 1).astype(jnp.int32),
            core,
            z,
            chip,
            owner_chip,
            row,
        ]
    )

    own, other, diag, one, two = prepare_call(panels, weight)
    got = lax.ppermute(diag, "xl", swap)
    sent, rows_b = small_call(
        choose_kernel, "choose", ((BLK, width), (weight.shape[0] // 2, BLK)), flags, own, lax.ppermute(other, "k", swap)
    )
    sent, got, diag, one, two = lax.optimization_barrier((sent, got, diag, one, two))
    came = lax.all_to_all(sent, CHIPS, 0, 0, tiled=True)
    diag = jnp.where(xl == (chip & 1), diag, got)
    got = lax.ppermute(diag, "z", [(i, i ^ 1) for i in range(4)])
    diag = jnp.where((z & 1) == ((chip >> 1) & 1), diag, got)
    got = lax.ppermute(diag, "z", [(i, i ^ 2) for i in range(4)])

    last_chip, last_core, last_row = N_CHIPS - 1, 1, N_ROWS - 1

    def down(value, bit, mask):
        rows = [r for r in range(N_ROWS) if (r ^ last_row) & ~mask == 0]
        at = functools.partial(device_at, last_chip, last_core)
        return lax.ppermute(value, AXES, [(at(r), at(r ^ bit)) for r in rows])

    one = jnp.where((row & 1) != 0, one, down(one, 1, 1))
    two = jnp.where((row & 4) != 0, two, down(two, 4, 4))
    (small,) = small_call(join_kernel, "join", ((weight.shape[0] // 2 + BLK, BLK),), flags, rows_b, diag, got)
    came, one, two, small = lax.optimization_barrier((came, one, two, small))
    got_one, got_two = down(one, 2, 3), down(two, 2, 6)

    pairs = [
        (device_at(d, k, r), device_at(r, k, d)) for d in range(N_CHIPS) for k in range(2) for r in range(N_ROWS)
    ]
    turned = lax.ppermute(lax.dynamic_slice_in_dim(came, owner_chip * piece, piece, 0), AXES, pairs)
    got = lax.ppermute(small, "xh", swap)
    small = jnp.where((chip & 4) == (owner_chip & 4), small, got)
    (copies,) = small_call(copies_kernel, "copies", ((N_ROWS, piece, width),), flags, turned)
    copies, small, got_one, got_two = lax.optimization_barrier((copies, small, got_one, got_two))
    panel0 = lax.all_to_all(copies, ROWS, 0, 0, tiled=True).reshape(BLK, width)
    got = lax.ppermute(small, "y", [(i, i ^ 1) for i in range(4)])
    small = jnp.where((chip & 1) == (owner_chip & 1), small, got)
    one = jnp.where((row & 2) != 0, one, got_one)
    two = jnp.where((row & 2) != 0, two, got_two)
    small, one, two = lax.optimization_barrier((small, one, two))
    got_one, got_two = down(one, 4, 7), down(two, 1, 7)
    got = lax.ppermute(small, "y", [(i, i ^ 2) for i in range(4)])
    small = jnp.where((chip & 2) == (owner_chip & 2), small, got)
    panel0, small = lax.optimization_barrier((panel0, small))
    other = lax.ppermute(small, "k", swap)

    wide_scales = scales[None, :]
    error, rounded = first_call(flags, grid_codes, small, other, wide_scales, block_inverse[0])
    return last_call(flags, grid_codes, weight, rounded, error, panel0, (one, got_one, two, got_two), wide_scales, block_inverse[1])


def solution(mesh):
    torus = Mesh(mesh.devices.reshape(SIZES), AXES)
    return jax.shard_map(
        local,
        mesh=torus,
        in_specs=(P(ROWS, COLS), P(ROWS), P(COLS, ROWS), P(), P(), P()),
        out_specs=P(ROWS, COLS),
        check_vma=False,
    )
```

```python
import functools

import jax
import jax.numpy as jnp
from jax import lax
from jax.experimental import pallas as pl
from jax.experimental.pallas import tpu as pltpu
from jax.sharding import Mesh
from jax.sharding import PartitionSpec as P

BLK = 128
SUB = 32
LEVELS = 16
softness = 0.2

SIZES = (2, 4, 2, 4, 2)
AXES = ("xh", "y", "k", "z", "xl")
COLS = ("xh", "y", "k")
ROWS = ("z", "xl")
CHIPS = ("xh", "y")
N_CHIPS = 8
N_ROWS = 8
LANES = 256
VMEM = 16 * 1024 * 1024
WIDE_VMEM = 51 * 1024 * 1024
BIG_VMEM = 54 * 1024 * 1024


def dot(a, b):
    return jnp.dot(a, b, precision=lax.Precision.HIGHEST, preferred_element_type=jnp.float32)


def fast_dot(a, b):
    return jnp.dot(a, b, preferred_element_type=jnp.float32)


def split(value):
    high = value.astype(jnp.bfloat16)
    low = (value - high.astype(jnp.float32)).astype(jnp.bfloat16)
    return high, low


def quantize(values, steps, inverse_steps, codes):
    levels = [codes[i].astype(jnp.float32) for i in range(LEVELS)]
    scaled = values * (inverse_steps * (0.5 / softness))
    output = jnp.full(values.shape, 0.5 * (levels[0] + levels[-1]), jnp.float32)
    for i in range(LEVELS - 1):
        half_gap = 0.5 * (levels[i + 1] - levels[i])
        shift = (levels[i] + levels[i + 1]) * (0.25 / softness)
        output = output + half_gap * jnp.tanh(scaled - shift)
    return output * steps


def inner_block(parts, steps, diag, inverse, codes):
    diag_t, inverse_t = diag.T, inverse.T
    rounded = [[] for _ in parts]
    errors = [[] for _ in parts]
    parts = list(parts)
    recip = [1.0 / s for s in steps]
    for g in range(BLK // SUB):
        low = g * SUB
        inv_g = inverse_t[low : low + SUB, low : low + SUB]
        later = diag_t[low + SUB :, low : low + SUB]
        for i, part in enumerate(parts):
            current = part[:SUB]
            quantized = quantize(current, steps[i], recip[i], codes)
            error = dot(inv_g, current - quantized)
            rounded[i].append(quantized)
            errors[i].append(error)
            if low + SUB < BLK:
                parts[i] = part[SUB:] - dot(later, error)
    return [jnp.concatenate(r, 0) for r in rounded], [jnp.concatenate(e, 0) for e in errors]


def transposed_parts(tiles):
    per = LANES // BLK
    turned = [t.T for t in tiles]
    return [jnp.concatenate(turned[i : i + per], 1) for i in range(0, len(turned), per)]


def first_kernel(flags, codes, small_ref, other_ref, scales_ref, inverse_ref, error_ref, rounded_ref):
    core, mine = flags[4], flags[0]
    half = scales_ref.shape[1] // 2
    parts, steps, places = [], [], []
    for ref, side in ((small_ref, core), (other_ref, 1 - core)):
        tiles = [ref[i : i + BLK, :] for i in range(0, half, BLK)]
        for i, part in enumerate(transposed_parts(tiles)):
            place = pl.multiple_of(side * half + i * LANES, LANES)
            parts.append(part)
            places.append(place)
            steps.append(scales_ref[:, pl.ds(place, LANES)])
    diag = jnp.where(mine == 1, small_ref[half:, :], other_ref[half:, :])
    rounded, errors = inner_block(parts, steps, diag, inverse_ref[...], codes)
    for i, place in enumerate(places):
        rows = pl.ds(place, LANES)
        rounded_ref[rows, :] = rounded[i].T
        high, low = split(errors[i].T)
        error_ref[rows, :BLK] = high
        error_ref[rows, BLK:] = low


def prepare_kernel(panel_ref, block_ref, own_ref, other_ref, diag_ref, one_ref, two_ref):
    core = lax.axis_index("k")
    last = (lax.axis_index("xh") * 4 + lax.axis_index("y")) * 2 + core == 2 * N_CHIPS - 1
    width, half = panel_ref.shape[1] // 2, block_ref.shape[0] // 2

    @pl.when(last)
    def _():
        one_ref[...] = panel_ref[:, width : width + width // 2]
        two_ref[...] = panel_ref[:, width + width // 2 :]

    piece = BLK // N_CHIPS
    for side in range(2):

        @pl.when(core == side)
        def _():
            diag_ref[...] = panel_ref[:, side * width : side * width + BLK]
            for ref, take in ((own_ref, side), (other_ref, 1 - side)):
                ref[:, :width] = panel_ref[:, take * width : (take + 1) * width]
                for q in range(half // BLK):
                    row = take * half + q * BLK
                    ref[:, width + q * BLK : width + (q + 1) * BLK] = block_ref[row : row + BLK, :]


def join_kernel(flags, rows_ref, diag_ref, got_ref, small_ref):
    z, chip = flags[5], flags[6]
    near = lax.div(z, 2) == lax.div(chip, 4)
    n = rows_ref.shape[0]
    small_ref[:n, :] = rows_ref[...]
    small_ref[n:, :] = jnp.where(near, diag_ref[...], got_ref[...])


def copies_kernel(flags, piece_ref, spread_ref):
    for e in range(N_ROWS):
        spread_ref[e] = piece_ref[...]


def choose_kernel(flags, own_ref, got_ref, panel_ref, rows_ref):
    mine, width = flags[0], panel_ref.shape[1]
    for value, ref in ((1, own_ref), (0, got_ref)):

        @pl.when(mine == value)
        def _():
            panel_ref[...] = ref[:, :width]
            for q in range(rows_ref.shape[0] // BLK):
                rows_ref[q * BLK : (q + 1) * BLK, :] = ref[:, width + q * BLK : width + (q + 1) * BLK]


def small_call(kernel, name, shapes, flags, *arrays, flops=0):
    smem, vmem = pl.BlockSpec(memory_space=pltpu.SMEM), pl.BlockSpec(memory_space=pltpu.VMEM)
    return pl.pallas_call(
        kernel,
        out_shape=tuple(jax.ShapeDtypeStruct(shape, jnp.float32) for shape in shapes),
        in_specs=[smem] + [vmem] * len(arrays),
        out_specs=(vmem,) * len(shapes),
        compiler_params=pltpu.CompilerParams(vmem_limit_bytes=VMEM),
        cost_estimate=pl.CostEstimate(flops=flops, bytes_accessed=10**5, transcendentals=0),
        name=name,
    )(flags, *arrays)


def prepare_call(panels, weight):
    n, wide = panels.shape
    rows = weight.shape[0]
    tall = wide // 2 + rows // 2
    whole = lambda shape: pl.BlockSpec(shape, lambda i: (0, 0))
    return pl.pallas_call(
        prepare_kernel,
        grid=(1,),
        out_shape=tuple(jax.ShapeDtypeStruct(s, jnp.float32) for s in ((n, tall), (n, tall), (n, BLK), (n, wide // 4), (n, wide // 4))),
        in_specs=[whole((n, wide)), whole((rows, BLK))],
        out_specs=(whole((n, tall)), whole((n, tall)), whole((n, BLK)), whole((n, wide // 4)), whole((n, wide // 4))),
        compiler_params=pltpu.CompilerParams(vmem_limit_bytes=BIG_VMEM),
        name="halves",
    )(panels, weight)


def last_kernel(
    flags, codes, weight_hbm, rounded_ref, error_ref, panel_ref, one_hbm, got_one_hbm, two_hbm, got_two_hbm, scales_ref, inverse_ref,
    out_ref, m_ref, error1_ref, rounded1_ref, weight_ref, arrived, panel1_ref, block_ref, down_done,
):
    step = pl.program_id(0)
    after, owner, last = flags[1], flags[2], flags[3]
    rows = out_ref.shape[0]

    def read(i):
        span = pl.ds(pl.multiple_of(i * rows, rows), rows)
        return pltpu.make_async_copy(weight_hbm.at[span, :], weight_ref.at[span, :], arrived.at[i])

    block_read = pltpu.make_async_copy(weight_hbm.at[:, :BLK], block_ref, down_done.at[1])

    @pl.when(jnp.logical_and(step == 0, last == 1))
    def _():
        block_read.start()

    half = out_ref.shape[1] // 2
    left, right = panel1_ref.at[:, :half], panel1_ref.at[:, half:]
    for bit, kept, got, place, at in ((4, one_hbm, got_one_hbm, left, 0), (1, two_hbm, got_two_hbm, right, 2)):
        for held, source in ((True, kept), (False, got)):

            @pl.when(jnp.logical_and(jnp.logical_and(step == 0, last == 1), ((flags[8] & bit) != 0) == held))
            def _():
                pltpu.make_async_copy(source, place, down_done.at[at]).start()

    @pl.when(step == 0)
    def _():
        for i in range(weight_hbm.shape[0] // rows):
            read(i).start()

    span0 = slice(0, 3 * BLK)

    def stage(source, masked, base):
        value = source[...]
        ids = lax.broadcasted_iota(jnp.int32, value.shape, 1)
        value = jnp.where(jnp.logical_and(masked == 1, ids < BLK), 0.0, value)
        high, low = split(value)
        for i, part in enumerate((high, high, low)):
            m_ref[base + i * BLK : base + (i + 1) * BLK, :] = part

    def three(error):
        return [error, error[:, :BLK]]

    @pl.when(jnp.logical_and(step == 0, after == 1))
    def _():
        stage(panel_ref, owner, 0)

    @pl.when(jnp.logical_and(step == 0, last == 1))
    def _():
        pltpu.make_async_copy(one_hbm, left, down_done.at[0]).wait()
        pltpu.make_async_copy(two_hbm, right, down_done.at[2]).wait()
        block_read.wait()
        block = block_ref[...] - fast_dot(jnp.concatenate(three(error_ref[...]), 1), m_ref[span0, :BLK])
        tiles = [block[i * BLK : (i + 1) * BLK] for i in range(block.shape[0] // BLK)]
        parts = transposed_parts(tiles)
        steps = [scales_ref[:, i * LANES : (i + 1) * LANES] for i in range(len(parts))]
        rounded, errors = inner_block(parts, steps, panel1_ref[:, :BLK], inverse_ref[...], codes)
        for i in range(len(parts)):
            span = slice(i * LANES, (i + 1) * LANES)
            rounded1_ref[span, :] = rounded[i].T
            high, low = split(errors[i].T)
            error1_ref[span, :BLK] = high
            error1_ref[span, BLK:] = low
        stage(panel1_ref, last, 3 * BLK)

    here = pl.ds(pl.multiple_of(step * rows, rows), rows)
    read(step).wait()

    @pl.when(after == 0)
    def _():
        out_ref[...] = weight_ref[here, :]

    @pl.when(jnp.logical_and(after == 1, last == 0))
    def _():
        error = jnp.concatenate(three(error_ref[here, :]), 1)
        out_ref[...] = weight_ref[here, :] - fast_dot(error, m_ref[span0, :])

    @pl.when(last == 1)
    def _():
        error = jnp.concatenate(three(error_ref[here, :]) + three(error1_ref[here, :]), 1)
        out_ref[...] = weight_ref[here, :] - fast_dot(error, m_ref[...])
        out_ref[:, :BLK] = rounded1_ref[here, :]

    @pl.when(owner == 1)
    def _():
        out_ref[:, :BLK] = rounded_ref[here, :]


def first_call(flags, codes, small, other, scales, inverse):
    n = scales.shape[1]
    smem, vmem = pl.BlockSpec(memory_space=pltpu.SMEM), pl.BlockSpec(memory_space=pltpu.VMEM)
    return pl.pallas_call(
        first_kernel,
        out_shape=(jax.ShapeDtypeStruct((n, 2 * BLK), jnp.bfloat16), jax.ShapeDtypeStruct((n, BLK), jnp.float32)),
        in_specs=[smem, smem, vmem, vmem, vmem, vmem],
        out_specs=(vmem, vmem),
        compiler_params=pltpu.CompilerParams(vmem_limit_bytes=VMEM),
        cost_estimate=pl.CostEstimate(flops=0, bytes_accessed=10**5, transcendentals=0),
        name="round_first",
    )(flags, codes, small, other, scales, inverse)


def last_call(flags, codes, weight, rounded, error, panel, panel1, scales, inverse):
    n, width = weight.shape
    rows = 256
    smem, vmem = pl.BlockSpec(memory_space=pltpu.SMEM), pl.BlockSpec(memory_space=pltpu.VMEM)
    tall, hbm = pl.BlockSpec((rows, width), lambda i: (i, 0)), pl.BlockSpec(memory_space=pltpu.HBM)
    return pl.pallas_call(
        last_kernel,
        grid=(n // rows,),
        out_shape=jax.ShapeDtypeStruct((n, width), jnp.float32),
        in_specs=[smem, smem, hbm] + [vmem] * 3 + [hbm] * 4 + [vmem] * 2,
        out_specs=tall,
        scratch_shapes=[
            pltpu.VMEM((6 * BLK, width), jnp.bfloat16),
            pltpu.VMEM((n, 2 * BLK), jnp.bfloat16),
            pltpu.VMEM((n, BLK), jnp.float32),
            pltpu.VMEM((n, width), jnp.float32),
            pltpu.SemaphoreType.DMA((n // rows,)),
            pltpu.VMEM((BLK, width), jnp.float32),
            pltpu.VMEM((n, BLK), jnp.float32),
            pltpu.SemaphoreType.DMA((3,)),
        ],
        compiler_params=pltpu.CompilerParams(vmem_limit_bytes=WIDE_VMEM),
        cost_estimate=pl.CostEstimate(flops=2 * 10**9, bytes_accessed=16 * 10**6, transcendentals=2 * 10**6),
        name="update_all",
    )(flags, codes, weight, rounded, error, panel, *panel1, scales, inverse)


def device_at(chip, core, row):
    return (chip * 2 + core) * N_ROWS + row


def local(weight, scales, panels, block_inverse, grid_codes, block_starts):
    width = weight.shape[1]
    xh, y, core, z, xl = (lax.axis_index(a) for a in AXES)
    chip = xh * 4 + y
    row = z * 2 + xl
    col = chip * 2 + core
    owner = block_starts[0] // width
    owner_chip, owner_core = owner // 2, owner % 2
    mine = core == owner_core
    piece = BLK // N_CHIPS
    swap = [(0, 1), (1, 0)]
    flags = jnp.stack(
        [
            mine.astype(jnp.int32),
            (col >= owner).astype(jnp.int32),
            (col == owner).astype(jnp.int32),
            (col == 2 * N_CHIPS - 1).astype(jnp.int32),
            core,
            z,
            chip,
            owner_chip,
            row,
        ]
    )

    own, other, diag, one, two = prepare_call(panels, weight)
    got = lax.ppermute(diag, "xl", swap)
    sent, rows_b = small_call(
        choose_kernel, "choose", ((BLK, width), (weight.shape[0] // 2, BLK)), flags, own, lax.ppermute(other, "k", swap)
    )
    sent, got, diag, one, two = lax.optimization_barrier((sent, got, diag, one, two))
    came = lax.all_to_all(sent, CHIPS, 0, 0, tiled=True)
    diag = jnp.where(xl == (chip & 1), diag, got)
    got = lax.ppermute(diag, "z", [(i, i ^ 1) for i in range(4)])
    diag = jnp.where((z & 1) == ((chip >> 1) & 1), diag, got)
    got = lax.ppermute(diag, "z", [(i, i ^ 2) for i in range(4)])

    last_chip, last_core, last_row = N_CHIPS - 1, 1, N_ROWS - 1

    def down(value, bit, mask):
        rows = [r for r in range(N_ROWS) if (r ^ last_row) & ~mask == 0]
        at = functools.partial(device_at, last_chip, last_core)
        return lax.ppermute(value, AXES, [(at(r), at(r ^ bit)) for r in rows])

    one = jnp.where((row & 1) != 0, one, down(one, 1, 1))
    two = jnp.where((row & 4) != 0, two, down(two, 4, 4))
    (small,) = small_call(join_kernel, "join", ((weight.shape[0] // 2 + BLK, BLK),), flags, rows_b, diag, got)
    came, one, two, small = lax.optimization_barrier((came, one, two, small))
    got_one, got_two = down(one, 2, 3), down(two, 2, 6)

    pairs = [
        (device_at(d, k, r), device_at(r, k, d)) for d in range(N_CHIPS) for k in range(2) for r in range(N_ROWS)
    ]
    turned = lax.ppermute(lax.dynamic_slice_in_dim(came, owner_chip * piece, piece, 0), AXES, pairs)
    got = lax.ppermute(small, "xh", swap)
    small = jnp.where((chip & 4) == (owner_chip & 4), small, got)
    (copies,) = small_call(copies_kernel, "copies", ((N_ROWS, piece, width),), flags, turned)
    copies, small, got_one, got_two = lax.optimization_barrier((copies, small, got_one, got_two))
    panel0 = lax.all_to_all(copies, ROWS, 0, 0, tiled=True).reshape(BLK, width)
    got = lax.ppermute(small, "y", [(i, i ^ 1) for i in range(4)])
    small = jnp.where((chip & 1) == (owner_chip & 1), small, got)
    one = jnp.where((row & 2) != 0, one, got_one)
    two = jnp.where((row & 2) != 0, two, got_two)
    small, one, two = lax.optimization_barrier((small, one, two))
    got_one, got_two = down(one, 4, 7), down(two, 1, 7)
    got = lax.ppermute(small, "y", [(i, i ^ 2) for i in range(4)])
    small = jnp.where((chip & 2) == (owner_chip & 2), small, got)
    panel0, small = lax.optimization_barrier((panel0, small))
    other = lax.ppermute(small, "k", swap)

    wide_scales = scales[None, :]
    error, rounded = first_call(flags, grid_codes, small, other, wide_scales, block_inverse[0])
    return last_call(flags, grid_codes, weight, rounded, error, panel0, (one, got_one, two, got_two), wide_scales, block_inverse[1])


def solution(mesh):
    torus = Mesh(mesh.devices.reshape(SIZES), AXES)
    return jax.shard_map(
        local,
        mesh=torus,
        in_specs=(P(ROWS, COLS), P(ROWS), P(COLS, ROWS), P(), P(), P()),
        out_specs=P(ROWS, COLS),
        check_vma=False,
    )
```

```python
import functools

import jax
import jax.numpy as jnp
from jax import lax
from jax.experimental import pallas as pl
from jax.experimental.pallas import tpu as pltpu
from jax.sharding import Mesh
from jax.sharding import PartitionSpec as P

BLK = 128
SUB = 32
LEVELS = 16
softness = 0.2

SIZES = (2, 4, 2, 4, 2)
AXES = ("xh", "y", "k", "z", "xl")
COLS = ("xh", "y", "k")
ROWS = ("z", "xl")
CHIPS = ("xh", "y")
N_CHIPS = 8
N_ROWS = 8
LANES = 256
VMEM = 16 * 1024 * 1024
WIDE_VMEM = 51 * 1024 * 1024
BIG_VMEM = 54 * 1024 * 1024


def split3(value):
    high = value.astype(jnp.bfloat16)
    rest = value - high.astype(jnp.float32)
    middle = rest.astype(jnp.bfloat16)
    return high, middle, (rest - middle.astype(jnp.float32)).astype(jnp.bfloat16)


def left_side(value):
    h, m, l = split3(value)
    return jnp.concatenate([h, h, m, h, l, m], 1)


def right_side(value):
    h, m, l = split3(value)
    return jnp.concatenate([h, m, h, l, h, m], 0)


def fast_dot(a, b):
    return jnp.dot(a, b, preferred_element_type=jnp.float32)


def split(value):
    high = value.astype(jnp.bfloat16)
    low = (value - high.astype(jnp.float32)).astype(jnp.bfloat16)
    return high, low


def quantize(values, steps, inverse_steps, codes):
    levels = [codes[i].astype(jnp.float32) for i in range(LEVELS)]
    scaled = values * (inverse_steps * (0.5 / softness))
    output = jnp.full(values.shape, 0.5 * (levels[0] + levels[-1]), jnp.float32)
    for i in range(LEVELS - 1):
        half_gap = 0.5 * (levels[i + 1] - levels[i])
        shift = (levels[i] + levels[i + 1]) * (0.25 / softness)
        output = output + half_gap * jnp.tanh(scaled - shift)
    return output * steps


def inner_block(parts, steps, diag, inverse, codes):
    diag_t, inverse_t = diag.T, inverse.T
    rounded = [[] for _ in parts]
    errors = [[] for _ in parts]
    parts = list(parts)
    recip = [1.0 / s for s in steps]
    for g in range(BLK // SUB):
        low = g * SUB
        inv_g = left_side(inverse_t[low : low + SUB, low : low + SUB])
        if low + SUB < BLK:
            later = left_side(diag_t[low + SUB :, low : low + SUB])
        for i, part in enumerate(parts):
            current = part[:SUB]
            quantized = quantize(current, steps[i], recip[i], codes)
            error = fast_dot(inv_g, right_side(current - quantized))
            rounded[i].append(quantized)
            errors[i].append(error)
            if low + SUB < BLK:
                parts[i] = part[SUB:] - fast_dot(later, right_side(error))
    return [jnp.concatenate(r, 0) for r in rounded], [jnp.concatenate(e, 0) for e in errors]


def transposed_parts(tiles):
    per = LANES // BLK
    turned = [t.T for t in tiles]
    return [jnp.concatenate(turned[i : i + per], 1) for i in range(0, len(turned), per)]


def first_kernel(flags, codes, small_ref, other_ref, scales_ref, inverse_ref, error_ref, rounded_ref):
    core, mine = flags[4], flags[0]
    half = scales_ref.shape[1] // 2
    parts, steps, places = [], [], []
    for ref, side in ((small_ref, core), (other_ref, 1 - core)):
        tiles = [ref[i : i + BLK, :] for i in range(0, half, BLK)]
        for i, part in enumerate(transposed_parts(tiles)):
            place = pl.multiple_of(side * half + i * LANES, LANES)
            parts.append(part)
            places.append(place)
            steps.append(scales_ref[:, pl.ds(place, LANES)])
    diag = jnp.where(mine == 1, small_ref[half:, :], other_ref[half:, :])
    rounded, errors = inner_block(parts, steps, diag, inverse_ref[...], codes)
    for i, place in enumerate(places):
        rows = pl.ds(place, LANES)
        rounded_ref[rows, :] = rounded[i].T
        high, low = split(errors[i].T)
        error_ref[rows, :BLK] = high
        error_ref[rows, BLK:] = low


def prepare_kernel(panel_ref, block_ref, own_ref, other_ref, diag_ref, one_ref, two_ref):
    core = lax.axis_index("k")
    last = (lax.axis_index("xh") * 4 + lax.axis_index("y")) * 2 + core == 2 * N_CHIPS - 1
    width, half = panel_ref.shape[1] // 2, block_ref.shape[0] // 2

    @pl.when(last)
    def _():
        one_ref[...] = panel_ref[:, width : width + width // 2]
        two_ref[...] = panel_ref[:, width + width // 2 :]

    piece = BLK // N_CHIPS
    for side in range(2):

        @pl.when(core == side)
        def _():
            diag_ref[...] = panel_ref[:, side * width : side * width + BLK]
            for ref, take in ((own_ref, side), (other_ref, 1 - side)):
                ref[:, :width] = panel_ref[:, take * width : (take + 1) * width]
                for q in range(half // BLK):
                    row = take * half + q * BLK
                    ref[:, width + q * BLK : width + (q + 1) * BLK] = block_ref[row : row + BLK, :]


def join_kernel(flags, rows_ref, diag_ref, got_ref, small_ref):
    z, chip = flags[5], flags[6]
    near = lax.div(z, 2) == lax.div(chip, 4)
    n = rows_ref.shape[0]
    small_ref[:n, :] = rows_ref[...]
    small_ref[n:, :] = jnp.where(near, diag_ref[...], got_ref[...])


def copies_kernel(flags, piece_ref, spread_ref):
    for e in range(N_ROWS):
        spread_ref[e] = piece_ref[...]


def choose_kernel(flags, own_ref, got_ref, panel_ref, rows_ref):
    mine, width = flags[0], panel_ref.shape[1]
    for value, ref in ((1, own_ref), (0, got_ref)):

        @pl.when(mine == value)
        def _():
            panel_ref[...] = ref[:, :width]
            for q in range(rows_ref.shape[0] // BLK):
                rows_ref[q * BLK : (q + 1) * BLK, :] = ref[:, width + q * BLK : width + (q + 1) * BLK]


def small_call(kernel, name, shapes, flags, *arrays, flops=0):
    smem, vmem = pl.BlockSpec(memory_space=pltpu.SMEM), pl.BlockSpec(memory_space=pltpu.VMEM)
    return pl.pallas_call(
        kernel,
        out_shape=tuple(jax.ShapeDtypeStruct(shape, jnp.float32) for shape in shapes),
        in_specs=[smem] + [vmem] * len(arrays),
        out_specs=(vmem,) * len(shapes),
        compiler_params=pltpu.CompilerParams(vmem_limit_bytes=VMEM),
        cost_estimate=pl.CostEstimate(flops=flops, bytes_accessed=10**5, transcendentals=0),
        name=name,
    )(flags, *arrays)


def prepare_call(panels, weight):
    n, wide = panels.shape
    rows = weight.shape[0]
    tall = wide // 2 + rows // 2
    whole = lambda shape: pl.BlockSpec(shape, lambda i: (0, 0))
    return pl.pallas_call(
        prepare_kernel,
        grid=(1,),
        out_shape=tuple(jax.ShapeDtypeStruct(s, jnp.float32) for s in ((n, tall), (n, tall), (n, BLK), (n, wide // 4), (n, wide // 4))),
        in_specs=[whole((n, wide)), whole((rows, BLK))],
        out_specs=(whole((n, tall)), whole((n, tall)), whole((n, BLK)), whole((n, wide // 4)), whole((n, wide // 4))),
        compiler_params=pltpu.CompilerParams(vmem_limit_bytes=BIG_VMEM),
        name="halves",
    )(panels, weight)


def last_kernel(
    flags, codes, weight_hbm, rounded_ref, error_ref, panel_ref, one_hbm, got_one_hbm, two_hbm, got_two_hbm, scales_ref, inverse_ref,
    out_ref, m_ref, error1_ref, rounded1_ref, weight_ref, arrived, panel1_ref, block_ref, down_done,
):
    step = pl.program_id(0)
    after, owner, last = flags[1], flags[2], flags[3]
    rows = out_ref.shape[0]

    def read(i):
        span = pl.ds(pl.multiple_of(i * rows, rows), rows)
        return pltpu.make_async_copy(weight_hbm.at[span, :], weight_ref.at[span, :], arrived.at[i])

    block_read = pltpu.make_async_copy(weight_hbm.at[:, :BLK], block_ref, down_done.at[1])

    @pl.when(jnp.logical_and(step == 0, last == 1))
    def _():
        block_read.start()

    half = out_ref.shape[1] // 2
    left, right = panel1_ref.at[:, :half], panel1_ref.at[:, half:]
    for bit, kept, got, place, at in ((4, one_hbm, got_one_hbm, left, 0), (1, two_hbm, got_two_hbm, right, 2)):
        for held, source in ((True, kept), (False, got)):

            @pl.when(jnp.logical_and(jnp.logical_and(step == 0, last == 1), ((flags[8] & bit) != 0) == held))
            def _():
                pltpu.make_async_copy(source, place, down_done.at[at]).start()

    @pl.when(step == 0)
    def _():
        for i in range(weight_hbm.shape[0] // rows):
            read(i).start()

    span0 = slice(0, 3 * BLK)

    def stage(source, masked, base):
        value = source[...]
        ids = lax.broadcasted_iota(jnp.int32, value.shape, 1)
        value = jnp.where(jnp.logical_and(masked == 1, ids < BLK), 0.0, value)
        high, low = split(value)
        for i, part in enumerate((high, high, low)):
            m_ref[base + i * BLK : base + (i + 1) * BLK, :] = part

    def three(error):
        return [error, error[:, :BLK]]

    @pl.when(jnp.logical_and(step == 0, after == 1))
    def _():
        stage(panel_ref, owner, 0)

    @pl.when(jnp.logical_and(step == 0, last == 1))
    def _():
        pltpu.make_async_copy(one_hbm, left, down_done.at[0]).wait()
        pltpu.make_async_copy(two_hbm, right, down_done.at[2]).wait()
        block_read.wait()
        block = block_ref[...] - fast_dot(jnp.concatenate(three(error_ref[...]), 1), m_ref[span0, :BLK])
        tiles = [block[i * BLK : (i + 1) * BLK] for i in range(block.shape[0] // BLK)]
        parts = transposed_parts(tiles)
        steps = [scales_ref[:, i * LANES : (i + 1) * LANES] for i in range(len(parts))]
        rounded, errors = inner_block(parts, steps, panel1_ref[:, :BLK], inverse_ref[...], codes)
        for i in range(len(parts)):
            span = slice(i * LANES, (i + 1) * LANES)
            rounded1_ref[span, :] = rounded[i].T
            high, low = split(errors[i].T)
            error1_ref[span, :BLK] = high
            error1_ref[span, BLK:] = low
        stage(panel1_ref, last, 3 * BLK)

    here = pl.ds(pl.multiple_of(step * rows, rows), rows)
    read(step).wait()

    @pl.when(after == 0)
    def _():
        out_ref[...] = weight_ref[here, :]

    @pl.when(jnp.logical_and(after == 1, last == 0))
    def _():
        error = jnp.concatenate(three(error_ref[here, :]), 1)
        out_ref[...] = weight_ref[here, :] - fast_dot(error, m_ref[span0, :])

    @pl.when(last == 1)
    def _():
        error = jnp.concatenate(three(error_ref[here, :]) + three(error1_ref[here, :]), 1)
        out_ref[...] = weight_ref[here, :] - fast_dot(error, m_ref[...])
        out_ref[:, :BLK] = rounded1_ref[here, :]

    @pl.when(owner == 1)
    def _():
        out_ref[:, :BLK] = rounded_ref[here, :]


def first_call(flags, codes, small, other, scales, inverse):
    n = scales.shape[1]
    smem, vmem = pl.BlockSpec(memory_space=pltpu.SMEM), pl.BlockSpec(memory_space=pltpu.VMEM)
    return pl.pallas_call(
        first_kernel,
        out_shape=(jax.ShapeDtypeStruct((n, 2 * BLK), jnp.bfloat16), jax.ShapeDtypeStruct((n, BLK), jnp.float32)),
        in_specs=[smem, smem, vmem, vmem, vmem, vmem],
        out_specs=(vmem, vmem),
        compiler_params=pltpu.CompilerParams(vmem_limit_bytes=VMEM),
        cost_estimate=pl.CostEstimate(flops=0, bytes_accessed=10**5, transcendentals=0),
        name="round_first",
    )(flags, codes, small, other, scales, inverse)


def last_call(flags, codes, weight, rounded, error, panel, panel1, scales, inverse):
    n, width = weight.shape
    rows = 256
    smem, vmem = pl.BlockSpec(memory_space=pltpu.SMEM), pl.BlockSpec(memory_space=pltpu.VMEM)
    tall, hbm = pl.BlockSpec((rows, width), lambda i: (i, 0)), pl.BlockSpec(memory_space=pltpu.HBM)
    return pl.pallas_call(
        last_kernel,
        grid=(n // rows,),
        out_shape=jax.ShapeDtypeStruct((n, width), jnp.float32),
        in_specs=[smem, smem, hbm] + [vmem] * 3 + [hbm] * 4 + [vmem] * 2,
        out_specs=tall,
        scratch_shapes=[
            pltpu.VMEM((6 * BLK, width), jnp.bfloat16),
            pltpu.VMEM((n, 2 * BLK), jnp.bfloat16),
            pltpu.VMEM((n, BLK), jnp.float32),
            pltpu.VMEM((n, width), jnp.float32),
            pltpu.SemaphoreType.DMA((n // rows,)),
            pltpu.VMEM((BLK, width), jnp.float32),
            pltpu.VMEM((n, BLK), jnp.float32),
            pltpu.SemaphoreType.DMA((3,)),
        ],
        compiler_params=pltpu.CompilerParams(vmem_limit_bytes=WIDE_VMEM),
        cost_estimate=pl.CostEstimate(flops=2 * 10**9, bytes_accessed=16 * 10**6, transcendentals=2 * 10**6),
        name="update_all",
    )(flags, codes, weight, rounded, error, panel, *panel1, scales, inverse)


def device_at(chip, core, row):
    return (chip * 2 + core) * N_ROWS + row


def local(weight, scales, panels, block_inverse, grid_codes, block_starts):
    width = weight.shape[1]
    xh, y, core, z, xl = (lax.axis_index(a) for a in AXES)
    chip = xh * 4 + y
    row = z * 2 + xl
    col = chip * 2 + core
    owner = block_starts[0] // width
    owner_chip, owner_core = owner // 2, owner % 2
    mine = core == owner_core
    piece = BLK // N_CHIPS
    swap = [(0, 1), (1, 0)]
    flags = jnp.stack(
        [
            mine.astype(jnp.int32),
            (col >= owner).astype(jnp.int32),
            (col == owner).astype(jnp.int32),
            (col == 2 * N_CHIPS - 1).astype(jnp.int32),
            core,
            z,
            chip,
            owner_chip,
            row,
        ]
    )

    own, other, diag, one, two = prepare_call(panels, weight)
    got = lax.ppermute(diag, "xl", swap)
    sent, rows_b = small_call(
        choose_kernel, "choose", ((BLK, width), (weight.shape[0] // 2, BLK)), flags, own, lax.ppermute(other, "k", swap)
    )
    sent, got, diag, one, two = lax.optimization_barrier((sent, got, diag, one, two))
    came = lax.all_to_all(sent, CHIPS, 0, 0, tiled=True)
    diag = jnp.where(xl == (chip & 1), diag, got)
    got = lax.ppermute(diag, "z", [(i, i ^ 1) for i in range(4)])
    diag = jnp.where((z & 1) == ((chip >> 1) & 1), diag, got)
    got = lax.ppermute(diag, "z", [(i, i ^ 2) for i in range(4)])

    last_chip, last_core, last_row = N_CHIPS - 1, 1, N_ROWS - 1

    def down(value, bit, mask):
        rows = [r for r in range(N_ROWS) if (r ^ last_row) & ~mask == 0]
        at = functools.partial(device_at, last_chip, last_core)
        return lax.ppermute(value, AXES, [(at(r), at(r ^ bit)) for r in rows])

    one = jnp.where((row & 1) != 0, one, down(one, 1, 1))
    two = jnp.where((row & 4) != 0, two, down(two, 4, 4))
    (small,) = small_call(join_kernel, "join", ((weight.shape[0] // 2 + BLK, BLK),), flags, rows_b, diag, got)
    came, one, two, small = lax.optimization_barrier((came, one, two, small))
    got_one, got_two = down(one, 2, 3), down(two, 2, 6)

    pairs = [
        (device_at(d, k, r), device_at(r, k, d)) for d in range(N_CHIPS) for k in range(2) for r in range(N_ROWS)
    ]
    turned = lax.ppermute(lax.dynamic_slice_in_dim(came, owner_chip * piece, piece, 0), AXES, pairs)
    got = lax.ppermute(small, "xh", swap)
    small = jnp.where((chip & 4) == (owner_chip & 4), small, got)
    (copies,) = small_call(copies_kernel, "copies", ((N_ROWS, piece, width),), flags, turned)
    copies, small, got_one, got_two = lax.optimization_barrier((copies, small, got_one, got_two))
    panel0 = lax.all_to_all(copies, ROWS, 0, 0, tiled=True).reshape(BLK, width)
    got = lax.ppermute(small, "y", [(i, i ^ 1) for i in range(4)])
    small = jnp.where((chip & 1) == (owner_chip & 1), small, got)
    one = jnp.where((row & 2) != 0, one, got_one)
    two = jnp.where((row & 2) != 0, two, got_two)
    small, one, two = lax.optimization_barrier((small, one, two))
    got_one, got_two = down(one, 4, 7), down(two, 1, 7)
    got = lax.ppermute(small, "y", [(i, i ^ 2) for i in range(4)])
    small = jnp.where((chip & 2) == (owner_chip & 2), small, got)
    panel0, small = lax.optimization_barrier((panel0, small))
    other = lax.ppermute(small, "k", swap)

    wide_scales = scales[None, :]
    error, rounded = first_call(flags, grid_codes, small, other, wide_scales, block_inverse[0])
    return last_call(flags, grid_codes, weight, rounded, error, panel0, (one, got_one, two, got_two), wide_scales, block_inverse[1])


def solution(mesh):
    torus = Mesh(mesh.devices.reshape(SIZES), AXES)
    return jax.shard_map(
        local,
        mesh=torus,
        in_specs=(P(ROWS, COLS), P(ROWS), P(COLS, ROWS), P(), P(), P()),
        out_specs=P(ROWS, COLS),
        check_vma=False,
    )
```

```python
import functools

import jax
import jax.numpy as jnp
from jax import lax
from jax.experimental import pallas as pl
from jax.experimental.pallas import tpu as pltpu
from jax.sharding import Mesh
from jax.sharding import PartitionSpec as P

BLK = 128
SUB = 32
LEVELS = 16
softness = 0.2

SIZES = (2, 4, 2, 4, 2)
AXES = ("xh", "y", "k", "z", "xl")
COLS = ("xh", "y", "k")
ROWS = ("z", "xl")
CHIPS = ("xh", "y")
N_CHIPS = 8
N_ROWS = 8
LANES = 512
VMEM = 16 * 1024 * 1024
WIDE_VMEM = 51 * 1024 * 1024
BIG_VMEM = 54 * 1024 * 1024


def split3(value):
    high = value.astype(jnp.bfloat16)
    rest = value - high.astype(jnp.float32)
    middle = rest.astype(jnp.bfloat16)
    return high, middle, (rest - middle.astype(jnp.float32)).astype(jnp.bfloat16)


def left_side(value):
    h, m, l = split3(value)
    return jnp.concatenate([h, h, m, h, l, m], 1)


def right_side(value):
    h, m, l = split3(value)
    return jnp.concatenate([h, m, h, l, h, m], 0)


def fast_dot(a, b):
    return jnp.dot(a, b, preferred_element_type=jnp.float32)


def split(value):
    high = value.astype(jnp.bfloat16)
    low = (value - high.astype(jnp.float32)).astype(jnp.bfloat16)
    return high, low


def quantize(values, steps, inverse_steps, codes):
    levels = [codes[i].astype(jnp.float32) for i in range(LEVELS)]
    scaled = values * (inverse_steps * (0.5 / softness))
    output = jnp.full(values.shape, 0.5 * (levels[0] + levels[-1]), jnp.float32)
    for i in range(LEVELS - 1):
        half_gap = 0.5 * (levels[i + 1] - levels[i])
        shift = (levels[i] + levels[i + 1]) * (0.25 / softness)
        output = output + half_gap * jnp.tanh(scaled - shift)
    return output * steps


def inner_block(parts, steps, diag, inverse, codes):
    diag_t, inverse_t = diag.T, inverse.T
    rounded = [[] for _ in parts]
    errors = [[] for _ in parts]
    parts = list(parts)
    recip = [1.0 / s for s in steps]
    for g in range(BLK // SUB):
        low = g * SUB
        inv_g = left_side(inverse_t[low : low + SUB, low : low + SUB])
        if low + SUB < BLK:
            later = left_side(diag_t[low + SUB :, low : low + SUB])
        for i, part in enumerate(parts):
            current = part[:SUB]
            quantized = quantize(current, steps[i], recip[i], codes)
            error = fast_dot(inv_g, right_side(current - quantized))
            rounded[i].append(quantized)
            errors[i].append(error)
            if low + SUB < BLK:
                parts[i] = part[SUB:] - fast_dot(later, right_side(error))
    return [jnp.concatenate(r, 0) for r in rounded], [jnp.concatenate(e, 0) for e in errors]


def transposed_parts(tiles):
    per = LANES // BLK
    turned = [t.T for t in tiles]
    return [jnp.concatenate(turned[i : i + per], 1) for i in range(0, len(turned), per)]


def first_kernel(flags, codes, small_ref, other_ref, scales_ref, inverse_ref, error_ref, rounded_ref):
    core, mine = flags[4], flags[0]
    half = scales_ref.shape[1] // 2
    parts, steps, places = [], [], []
    for ref, side in ((small_ref, core), (other_ref, 1 - core)):
        tiles = [ref[i : i + BLK, :] for i in range(0, half, BLK)]
        for i, part in enumerate(transposed_parts(tiles)):
            place = pl.multiple_of(side * half + i * LANES, LANES)
            parts.append(part)
            places.append(place)
            steps.append(scales_ref[:, pl.ds(place, LANES)])
    diag = jnp.where(mine == 1, small_ref[half:, :], other_ref[half:, :])
    rounded, errors = inner_block(parts, steps, diag, inverse_ref[...], codes)
    for i, place in enumerate(places):
        rows = pl.ds(place, LANES)
        rounded_ref[rows, :] = rounded[i].T
        high, low = split(errors[i].T)
        error_ref[rows, :BLK] = high
        error_ref[rows, BLK:] = low


def prepare_kernel(panel_ref, block_ref, own_ref, other_ref, diag_ref, one_ref, two_ref):
    core = lax.axis_index("k")
    last = (lax.axis_index("xh") * 4 + lax.axis_index("y")) * 2 + core == 2 * N_CHIPS - 1
    width, half = panel_ref.shape[1] // 2, block_ref.shape[0] // 2

    @pl.when(last)
    def _():
        one_ref[...] = panel_ref[:, width : width + width // 2]
        two_ref[...] = panel_ref[:, width + width // 2 :]

    piece = BLK // N_CHIPS
    for side in range(2):

        @pl.when(core == side)
        def _():
            diag_ref[...] = panel_ref[:, side * width : side * width + BLK]
            for ref, take in ((own_ref, side), (other_ref, 1 - side)):
                ref[:, :width] = panel_ref[:, take * width : (take + 1) * width]
                for q in range(half // BLK):
                    row = take * half + q * BLK
                    ref[:, width + q * BLK : width + (q + 1) * BLK] = block_ref[row : row + BLK, :]


def join_kernel(flags, rows_ref, diag_ref, got_ref, small_ref):
    z, chip = flags[5], flags[6]
    near = lax.div(z, 2) == lax.div(chip, 4)
    n = rows_ref.shape[0]
    small_ref[:n, :] = rows_ref[...]
    small_ref[n:, :] = jnp.where(near, diag_ref[...], got_ref[...])


def choose_kernel(flags, own_ref, got_ref, panel_ref, rows_ref):
    mine, width = flags[0], panel_ref.shape[1]
    for value, ref in ((1, own_ref), (0, got_ref)):

        @pl.when(mine == value)
        def _():
            panel_ref[...] = ref[:, :width]
            for q in range(rows_ref.shape[0] // BLK):
                rows_ref[q * BLK : (q + 1) * BLK, :] = ref[:, width + q * BLK : width + (q + 1) * BLK]


def small_call(kernel, name, shapes, flags, *arrays, flops=0):
    smem, vmem = pl.BlockSpec(memory_space=pltpu.SMEM), pl.BlockSpec(memory_space=pltpu.VMEM)
    return pl.pallas_call(
        kernel,
        out_shape=tuple(jax.ShapeDtypeStruct(shape, jnp.float32) for shape in shapes),
        in_specs=[smem] + [vmem] * len(arrays),
        out_specs=(vmem,) * len(shapes),
        compiler_params=pltpu.CompilerParams(vmem_limit_bytes=VMEM),
        cost_estimate=pl.CostEstimate(flops=flops, bytes_accessed=10**5, transcendentals=0),
        name=name,
    )(flags, *arrays)


def prepare_call(panels, weight):
    n, wide = panels.shape
    rows = weight.shape[0]
    tall = wide // 2 + rows // 2
    whole = lambda shape: pl.BlockSpec(shape, lambda i: (0, 0))
    return pl.pallas_call(
        prepare_kernel,
        grid=(1,),
        out_shape=tuple(jax.ShapeDtypeStruct(s, jnp.float32) for s in ((n, tall), (n, tall), (n, BLK), (n, wide // 4), (n, wide // 4))),
        in_specs=[whole((n, wide)), whole((rows, BLK))],
        out_specs=(whole((n, tall)), whole((n, tall)), whole((n, BLK)), whole((n, wide // 4)), whole((n, wide // 4))),
        compiler_params=pltpu.CompilerParams(vmem_limit_bytes=BIG_VMEM),
        name="halves",
    )(panels, weight)


def last_kernel(
    flags, codes, weight_hbm, rounded_ref, error_ref, panel_ref, one_hbm, got_one_hbm, two_hbm, got_two_hbm, scales_ref, inverse_ref,
    out_ref, m_ref, error1_ref, rounded1_ref, weight_ref, arrived, panel1_ref, block_ref, down_done,
):
    step = pl.program_id(0)
    after, owner, last = flags[1], flags[2], flags[3]
    rows = out_ref.shape[0]

    def read(i):
        span = pl.ds(pl.multiple_of(i * rows, rows), rows)
        return pltpu.make_async_copy(weight_hbm.at[span, :], weight_ref.at[span, :], arrived.at[i])

    block_read = pltpu.make_async_copy(weight_hbm.at[:, :BLK], block_ref, down_done.at[1])

    @pl.when(jnp.logical_and(step == 0, last == 1))
    def _():
        block_read.start()

    half = out_ref.shape[1] // 2
    left, right = panel1_ref.at[:, :half], panel1_ref.at[:, half:]
    for bit, kept, got, place, at in ((4, one_hbm, got_one_hbm, left, 0), (1, two_hbm, got_two_hbm, right, 2)):
        for held, source in ((True, kept), (False, got)):

            @pl.when(jnp.logical_and(jnp.logical_and(step == 0, last == 1), ((flags[8] & bit) != 0) == held))
            def _():
                pltpu.make_async_copy(source, place, down_done.at[at]).start()

    @pl.when(step == 0)
    def _():
        for i in range(weight_hbm.shape[0] // rows):
            read(i).start()

    span0 = slice(0, 3 * BLK)

    def stage(source, masked, base):
        value = source[...]
        ids = lax.broadcasted_iota(jnp.int32, value.shape, 1)
        value = jnp.where(jnp.logical_and(masked == 1, ids < BLK), 0.0, value)
        high, low = split(value)
        for i, part in enumerate((high, high, low)):
            m_ref[base + i * BLK : base + (i + 1) * BLK, :] = part

    def three(error):
        return [error, error[:, :BLK]]

    @pl.when(jnp.logical_and(step == 0, after == 1))
    def _():
        stage(panel_ref, owner, 0)

    @pl.when(jnp.logical_and(step == 0, last == 1))
    def _():
        pltpu.make_async_copy(one_hbm, left, down_done.at[0]).wait()
        pltpu.make_async_copy(two_hbm, right, down_done.at[2]).wait()
        block_read.wait()
        block = block_ref[...] - fast_dot(jnp.concatenate(three(error_ref[...]), 1), m_ref[span0, :BLK])
        tiles = [block[i * BLK : (i + 1) * BLK] for i in range(block.shape[0] // BLK)]
        parts = transposed_parts(tiles)
        steps = [scales_ref[:, i * LANES : (i + 1) * LANES] for i in range(len(parts))]
        rounded, errors = inner_block(parts, steps, panel1_ref[:, :BLK], inverse_ref[...], codes)
        for i in range(len(parts)):
            span = slice(i * LANES, (i + 1) * LANES)
            rounded1_ref[span, :] = rounded[i].T
            high, low = split(errors[i].T)
            error1_ref[span, :BLK] = high
            error1_ref[span, BLK:] = low
        stage(panel1_ref, last, 3 * BLK)

    here = pl.ds(pl.multiple_of(step * rows, rows), rows)
    read(step).wait()

    @pl.when(after == 0)
    def _():
        out_ref[...] = weight_ref[here, :]

    @pl.when(jnp.logical_and(after == 1, last == 0))
    def _():
        error = jnp.concatenate(three(error_ref[here, :]), 1)
        out_ref[...] = weight_ref[here, :] - fast_dot(error, m_ref[span0, :])

    @pl.when(last == 1)
    def _():
        error = jnp.concatenate(three(error_ref[here, :]) + three(error1_ref[here, :]), 1)
        out_ref[...] = weight_ref[here, :] - fast_dot(error, m_ref[...])
        out_ref[:, :BLK] = rounded1_ref[here, :]

    @pl.when(owner == 1)
    def _():
        out_ref[:, :BLK] = rounded_ref[here, :]


def first_call(flags, codes, small, other, scales, inverse):
    n = scales.shape[1]
    smem, vmem = pl.BlockSpec(memory_space=pltpu.SMEM), pl.BlockSpec(memory_space=pltpu.VMEM)
    return pl.pallas_call(
        first_kernel,
        out_shape=(jax.ShapeDtypeStruct((n, 2 * BLK), jnp.bfloat16), jax.ShapeDtypeStruct((n, BLK), jnp.float32)),
        in_specs=[smem, smem, vmem, vmem, vmem, vmem],
        out_specs=(vmem, vmem),
        compiler_params=pltpu.CompilerParams(vmem_limit_bytes=VMEM),
        cost_estimate=pl.CostEstimate(flops=0, bytes_accessed=10**5, transcendentals=0),
        name="round_first",
    )(flags, codes, small, other, scales, inverse)


def last_call(flags, codes, weight, rounded, error, panel, panel1, scales, inverse):
    n, width = weight.shape
    rows = 256
    smem, vmem = pl.BlockSpec(memory_space=pltpu.SMEM), pl.BlockSpec(memory_space=pltpu.VMEM)
    tall, hbm = pl.BlockSpec((rows, width), lambda i: (i, 0)), pl.BlockSpec(memory_space=pltpu.HBM)
    return pl.pallas_call(
        last_kernel,
        grid=(n // rows,),
        out_shape=jax.ShapeDtypeStruct((n, width), jnp.float32),
        in_specs=[smem, smem, hbm] + [vmem] * 3 + [hbm] * 4 + [vmem] * 2,
        out_specs=tall,
        scratch_shapes=[
            pltpu.VMEM((6 * BLK, width), jnp.bfloat16),
            pltpu.VMEM((n, 2 * BLK), jnp.bfloat16),
            pltpu.VMEM((n, BLK), jnp.float32),
            pltpu.VMEM((n, width), jnp.float32),
            pltpu.SemaphoreType.DMA((n // rows,)),
            pltpu.VMEM((BLK, width), jnp.float32),
            pltpu.VMEM((n, BLK), jnp.float32),
            pltpu.SemaphoreType.DMA((3,)),
        ],
        compiler_params=pltpu.CompilerParams(vmem_limit_bytes=WIDE_VMEM),
        cost_estimate=pl.CostEstimate(flops=2 * 10**9, bytes_accessed=16 * 10**6, transcendentals=2 * 10**6),
        name="update_all",
    )(flags, codes, weight, rounded, error, panel, *panel1, scales, inverse)


def device_at(chip, core, row):
    return (chip * 2 + core) * N_ROWS + row


def local(weight, scales, panels, block_inverse, grid_codes, block_starts):
    width = weight.shape[1]
    xh, y, core, z, xl = (lax.axis_index(a) for a in AXES)
    chip = xh * 4 + y
    row = z * 2 + xl
    col = chip * 2 + core
    owner = block_starts[0] // width
    owner_chip, owner_core = owner // 2, owner % 2
    mine = core == owner_core
    piece = BLK // N_CHIPS
    swap = [(0, 1), (1, 0)]
    flags = jnp.stack(
        [
            mine.astype(jnp.int32),
            (col >= owner).astype(jnp.int32),
            (col == owner).astype(jnp.int32),
            (col == 2 * N_CHIPS - 1).astype(jnp.int32),
            core,
            z,
            chip,
            owner_chip,
            row,
        ]
    )

    own, other, diag, one, two = prepare_call(panels, weight)
    got = lax.ppermute(diag, "xl", swap)
    sent, rows_b = small_call(
        choose_kernel, "choose", ((BLK, width), (weight.shape[0] // 2, BLK)), flags, own, lax.ppermute(other, "k", swap)
    )
    sent, got, diag, one, two = lax.optimization_barrier((sent, got, diag, one, two))
    came = lax.all_to_all(sent, CHIPS, 0, 0, tiled=True)
    diag = jnp.where(xl == (chip & 1), diag, got)
    got = lax.ppermute(diag, "z", [(i, i ^ 1) for i in range(4)])
    diag = jnp.where((z & 1) == ((chip >> 1) & 1), diag, got)
    got = lax.ppermute(diag, "z", [(i, i ^ 2) for i in range(4)])

    last_chip, last_core, last_row = N_CHIPS - 1, 1, N_ROWS - 1

    def down(value, bit, mask):
        rows = [r for r in range(N_ROWS) if (r ^ last_row) & ~mask == 0]
        at = functools.partial(device_at, last_chip, last_core)
        return lax.ppermute(value, AXES, [(at(r), at(r ^ bit)) for r in rows])

    one = jnp.where((row & 1) != 0, one, down(one, 1, 1))
    two = jnp.where((row & 4) != 0, two, down(two, 4, 4))
    (small,) = small_call(join_kernel, "join", ((weight.shape[0] // 2 + BLK, BLK),), flags, rows_b, diag, got)
    came, one, two, small = lax.optimization_barrier((came, one, two, small))
    got_one, got_two = down(one, 2, 3), down(two, 2, 6)

    pairs = [
        (device_at(d, k, r), device_at(r, k, d)) for d in range(N_CHIPS) for k in range(2) for r in range(N_ROWS)
    ]
    turned = lax.ppermute(lax.dynamic_slice_in_dim(came, owner_chip * piece, piece, 0), AXES, pairs)
    got = lax.ppermute(small, "xh", swap)
    small = jnp.where((chip & 4) == (owner_chip & 4), small, got)
    copies = jnp.broadcast_to(turned, (N_ROWS, piece, width))
    copies, small, got_one, got_two = lax.optimization_barrier((copies, small, got_one, got_two))
    panel0 = lax.all_to_all(copies, ROWS, 0, 0, tiled=True).reshape(BLK, width)
    got = lax.ppermute(small, "y", [(i, i ^ 1) for i in range(4)])
    small = jnp.where((chip & 1) == (owner_chip & 1), small, got)
    one = jnp.where((row & 2) != 0, one, got_one)
    two = jnp.where((row & 2) != 0, two, got_two)
    small, one, two = lax.optimization_barrier((small, one, two))
    got_one, got_two = down(one, 4, 7), down(two, 1, 7)
    got = lax.ppermute(small, "y", [(i, i ^ 2) for i in range(4)])
    small = jnp.where((chip & 2) == (owner_chip & 2), small, got)
    panel0, small = lax.optimization_barrier((panel0, small))
    other = lax.ppermute(small, "k", swap)

    wide_scales = scales[None, :]
    error, rounded = first_call(flags, grid_codes, small, other, wide_scales, block_inverse[0])
    return last_call(flags, grid_codes, weight, rounded, error, panel0, (one, got_one, two, got_two), wide_scales, block_inverse[1])


def solution(mesh):
    torus = Mesh(mesh.devices.reshape(SIZES), AXES)
    return jax.shard_map(
        local,
        mesh=torus,
        in_specs=(P(ROWS, COLS), P(ROWS), P(COLS, ROWS), P(), P(), P()),
        out_specs=P(ROWS, COLS),
        check_vma=False,
    )
```
